32 devices in a mesh: replica: 2 (over y), dev: 8 (over z, x), pair: 2 (over core).
Axes of the slice: x: 2, y: 2, z: 4, core: 2. Of those that a mesh axis runs over, the one named last changes fastest.
Arguments:
- text_rows: bfloat16 [2048, 8192], P(('replica', 'dev'), 'pair'), parts along dimension 0, may hold values from -6 to 6
- vision_rows: bfloat16 [1024, 8192], P(('replica', 'dev'), 'pair'), parts along dimension 0, may hold values from -6 to 6
- vision_device: int32 [1024, 1], P(('replica', 'dev')), parts along dimension 0, may hold values from 0 to 7; in each aligned block of 64 rows (0 to 63, 64 to 127, ...) at most 16 rows name the same one
- vision_slot: int32 [1024], P(('replica', 'dev')), parts along dimension 0, may hold values from 0 to 127
- positions: int32 [2048], P(('replica', 'dev')), parts along dimension 0, may hold values from 0 to 1023, each once
- norm_gain: bfloat16 [8192], replicated, may hold values from 0.099609375 to 1.8984375
- kv_weight: bfloat16 [8192, 1024], P('dev', 'pair'), may hold values from -0.0625 to 0.0625
- kv_bias: bfloat16 [1024], P('pair'), may hold values from -3 to 3
- queries: bfloat16 [2048, 4096], P(('replica', 'dev'), 'pair'), parts along dimension 0
- page_table: int32 [16, 8], P(('replica', 'dev')), parts along dimension 0, may hold values from 0 to 7, each once within a row
Outputs:
- attended: bfloat16 [2048, 4096], P(('replica', 'dev'), 'pair'), parts along dimension 0
- kv_cache: bfloat16 [128, 16, 1024], P(('replica', 'dev'), None, 'pair'), parts along dimension 0
The draws below stay inside these ranges and needn't reach their ends.
There are 2 independent parts, one for each index of `replica`. The reference program is written for one: setup_inputs(seed, part) draws one part's arguments, and reference() takes and returns one part's arrays. A program takes and returns all parts, laid end to end along the dimension named above; an argument that names none is the same for every part. Nothing has to cross between parts.
Inputs may be any that keep to these rules, and one draw needn't show every extreme that they name: `vision_device`: among the vision rows of one index of dev at most 16 name the same index. `positions`: each prompt position appears once. `page_table`: each row names each of its 8 pages once.
All inputs are finite; a program needn't handle non-finite values.
Results may differ from the reference program's by a relative error of at most 0.0039.
The reference program's roundings to bfloat16 on the way (of `embedded`, `normed`, `kv` and `weights`) count: a program that leaves them out, or rounds other values in their place, can miss the bound.
Values may be sent and summed in bfloat16 or wider, within the bound.
A program may use at most 64 MiB of HBM per device.

```python
import math
import jax
import jax.numpy as jnp
import numpy as np
from jax import lax

D = 8192
QHEADS = 32
KVHEADS = 4
HD = 128
PAGE = 16
TOK_DEV = 128
VIS_DEV = 64
CAP = 16
SEQ_LEN = 1024
VIS = 512
PAGES_DEV = 8
N_DEV = 8


def draw_queries(key, part):
    key = jax.random.fold_in(key, 11)
    inner = jax.random.fold_in(key, 0)
    return jax.random.normal(inner, (SEQ_LEN, QHEADS * HD), jnp.float32).astype(jnp.bfloat16)


def touch_ends(result, rng, least, high):
    index_at = [jax.random.randint(jax.random.fold_in(rng, axis), (), 0, length) for axis, length in enumerate(result.shape)]
    widest = result.shape.index(max(result.shape))
    next_to = index_at[:widest] + [(index_at[widest] + 1) % result.shape[widest]] + index_at[widest + 1:]
    return result.at[tuple(index_at)].set(least).at[tuple(next_to)].set(high)


def level_of(stream_key, extent, shards, least, largest):
    gain, own = 1.0, jax.random.fold_in(stream_key, 6)
    for dim, parts in shards:
        heights = jnp.exp(jax.random.uniform(jax.random.fold_in(own, dim), (parts,), jnp.float32, least / len(shards), largest / len(shards)))
        gain = gain * jnp.repeat(heights, extent[dim] // parts).reshape([-1 if axis == dim else 1 for axis in range(len(extent))])
    return gain


def routed_block(rng, own, number, rows, number_of, top, reach, lean):
    ranking = jax.random.permutation(rng, number_of)
    packed, common = portions_of(number_of, rows * top, reach, lean, True), portions_of(number_of, rows * top, reach, lean, False)
    places = jnp.arange(number_of)

    def named(tallies, rotation):
        used = int((tallies > 0).sum())
        fixed = max(1, used // 4)
        passed = fixed + (places - fixed + rotation * (used - fixed)) % max(1, number_of - fixed)
        return jnp.zeros((number_of,), jnp.int32).at[ranking[jnp.where(places < fixed, places, passed)]].set(jnp.asarray(tallies, jnp.int32))

    tallies = jnp.where(number % 4 == 0, named(packed, number // 4), named(common, number - number // 4 - 1))
    mixed = jax.random.permutation(jax.random.fold_in(own, 3), number_of)
    donor, taker = mixed[0:number_of // 2 * 2:2], mixed[1:number_of // 2 * 2:2]
    room = jnp.minimum(tallies[donor] - 1, reach - tallies[taker]) // 2
    room = jnp.where((donor == ranking[0]) | (taker == ranking[0]) | (tallies[taker] == 0), 0, jnp.maximum(room, 0))
    passed = jax.random.randint(jax.random.fold_in(own, 4), (number_of // 2,), 0, 1 << 20) % (room + 1)
    tallies = tallies.at[donor].add(-passed).at[taker].add(passed)
    members = jnp.searchsorted(jnp.cumsum(tallies), jnp.arange(rows * top), side="right").astype(jnp.int32)
    table = members.reshape(top, rows).T
    table = table[jax.random.permutation(jax.random.fold_in(own, 1), rows)]
    rotation = jax.random.randint(jax.random.fold_in(own, 2), (rows, 1), 0, top)
    return jnp.take_along_axis(table, (jnp.arange(top)[None, :] + rotation) % top, axis=1)


def portions_of(amount, total, reach, skew, full):
    loads = [(1 << 20) // math.isqrt(rank ** skew) + 1 for rank in range(1, amount + 1)]
    largest = reach if full else min(reach, max(-(-total // amount), total * loads[0] // sum(loads)))
    least = 1 if total - largest >= amount - 1 else 0
    holding, surplus = [largest] + [least] * (amount - 1), total - largest - least * (amount - 1)
    while surplus > 0:
        candidates = [i for i in range(1, amount) if holding[i] < largest] or [i for i in range(1, amount) if holding[i] < reach]
        pool, remaining = sum([loads[i] for i in candidates]), surplus
        for i in candidates:
            addition = min(reach - holding[i], max(1, remaining * loads[i] // pool), surplus)
            holding[i] = holding[i] + addition
            surplus = surplus - addition
    return np.array(holding)


def bell_draw(rng, extent, deviation, reach, pieces=(), kind=jnp.bfloat16):
    gain = level_of(rng, extent, pieces, -0.22, 0.18) if pieces else 1.0
    entries = jax.random.normal(rng, extent, jnp.float32) * deviation * gain
    return jnp.minimum(jnp.maximum(entries, -reach), reach).astype(kind)


def setup_inputs(seed: int = 0, part: int = 0) -> dict:
    arg_keys = jax.random.split(jax.random.key(seed), 11)
    part_keys = jax.random.split(jax.random.fold_in(arg_keys[10], part), 11)
    text_rows = bell_draw(part_keys[0], (SEQ_LEN, D), 1.0, 6.0, ((0, 8), (1, 2)))
    vision_rows = bell_draw(part_keys[1], (VIS, D), 1.0, 6.0, ((0, 8), (1, 2)))
    vision_device_keys = jax.random.split(jax.random.fold_in(part_keys[2], 1), VIS // VIS_DEV)
    vision_device_turns = jax.random.permutation(jax.random.fold_in(part_keys[2], 3), VIS // VIS_DEV)
    vision_device = jax.vmap(lambda own, number: routed_block(jax.random.fold_in(part_keys[2], 2), own, number, VIS_DEV, N_DEV, 1, CAP, 2))(vision_device_keys, vision_device_turns).reshape((VIS, 1))
    vision_slot = touch_ends(jax.random.randint(part_keys[3], (VIS,), 0, TOK_DEV), jax.random.fold_in(part_keys[3], 1), 0, TOK_DEV - 1).astype(jnp.int32)
    positions = jax.random.permutation(part_keys[4], SEQ_LEN).astype(jnp.int32)
    norm_gain = jnp.clip(1.0 + 0.18 * jax.random.normal(arg_keys[5], (D,), jnp.float32), 0.099609375, 1.8984375).astype(jnp.bfloat16)
    kv_weight = bell_draw(arg_keys[6], (D, 2 * KVHEADS * HD), D ** -0.5, 0.0625, ((0, 8), (1, 2)))
    kv_bias = bell_draw(arg_keys[7], (2 * KVHEADS * HD,), 0.5, 3.0, ((0, 2),))
    queries = draw_queries(jax.random.fold_in(jax.random.fold_in(arg_keys[10], part), 71), part)
    page_table = jax.vmap(lambda own: jax.random.permutation(own, PAGES_DEV))(jax.random.split(part_keys[9], N_DEV)).reshape((N_DEV, PAGES_DEV)).astype(jnp.int32)
    return {"text_rows": text_rows, "vision_rows": vision_rows, "vision_device": vision_device, "vision_slot": vision_slot, "positions": positions, "norm_gain": norm_gain, "kv_weight": kv_weight, "kv_bias": kv_bias, "queries": queries, "page_table": page_table}


def attend(block_q, block_pos, keys, values, key_pos):
    scores = jnp.einsum('tkgd,skd->kgts', block_q.astype(jnp.float32), keys.astype(jnp.float32)) * HD ** (-0.5)
    allowed = key_pos[None, :] <= block_pos[:, None]
    peak = lax.optimization_barrier(jnp.max(jnp.where(allowed, scores, -1e+30), axis=-1))
    weights = jnp.where(allowed, jnp.exp(scores - peak[..., None]), 0.0)
    total = lax.optimization_barrier(jnp.sum(weights, axis=-1))
    mixed = jnp.einsum('kgts,skd->kgtd', weights.astype(jnp.bfloat16).astype(jnp.float32), values.astype(jnp.float32))
    mixed = mixed / total[..., None]
    rows = block_q.shape[0]
    return jnp.transpose(mixed, (2, 0, 1, 3)).reshape(rows, -1).astype(jnp.bfloat16)

def reference(text_rows, vision_rows, vision_device, vision_slot, positions, norm_gain, kv_weight, kv_bias, queries, page_table):
    target = (vision_device[:, 0] * TOK_DEV + vision_slot).astype(jnp.int32)
    added = jax.ops.segment_sum(vision_rows.astype(jnp.float32), target, num_segments=SEQ_LEN)
    embedded = (text_rows.astype(jnp.float32) + added).astype(jnp.bfloat16)
    floats = embedded.astype(jnp.float32)
    meansq = lax.optimization_barrier(jnp.mean(floats * floats, axis=-1, keepdims=True))
    normed = (floats * lax.rsqrt(meansq + 1e-06) * norm_gain.astype(jnp.float32)).astype(jnp.bfloat16)
    kv = (jnp.dot(normed, kv_weight, preferred_element_type=jnp.float32) + kv_bias.astype(jnp.float32)).astype(jnp.bfloat16)
    pages = kv.reshape(N_DEV, PAGES_DEV, PAGE, -1)
    kv_cache = jnp.take_along_axis(pages, page_table[:, :, None, None].astype(jnp.int32), axis=1).reshape(N_DEV * PAGES_DEV, PAGE, -1)
    split = kv.reshape(SEQ_LEN, KVHEADS, 2, HD)
    keys = split[:, :, 0]
    values = split[:, :, 1]
    group = QHEADS // KVHEADS
    block = math.gcd(SEQ_LEN, 256)
    query_blocks = queries.reshape(SEQ_LEN // block, block, KVHEADS, group, HD)
    pos_blocks = positions.reshape(SEQ_LEN // block, block)
    outputs = lax.map(lambda item: attend(item[0], item[1], keys, values, positions), (query_blocks, pos_blocks))
    attended = outputs.reshape(SEQ_LEN, QHEADS * HD)
    return (attended, kv_cache)
```

```python
import functools

import jax
import jax.numpy as jnp
from jax import lax
from jax.experimental import pallas as pl
from jax.experimental.pallas import tpu as pltpu
from jax.sharding import PartitionSpec as P

MESH = pl.DeviceIdType.MESH
HD = 128
PAGE = 16
LANES = 128
F32 = jnp.float32
BF16 = jnp.bfloat16


def ring_position(d, n):
    z, x = d // 2, d % 2
    return z * (1 - x) + (n - 1 - z) * x


def ring_device(r, n):
    back = r // (n // 2)
    return (1 - back) * 2 * r + back * (2 * (n - 1 - r) + 1)


def kernel(
    n,
    cap,
    text_ref,
    vision_ref,
    dest_row_ref,
    dest_col_ref,
    slot_col_ref,
    pos_row_ref,
    pos_col_ref,
    gain_ref,
    weight_ref,
    bias_ref,
    query_ref,
    page_ref,
    out_ref,
    cache_ref,
    wbuf,
    vsend,
    vrecv,
    msend,
    mrecv,
    emb,
    nbuf,
    kvbuf,
    mask,
    local_sem,
    wsend_sem,
    wrecv_sem,
    ysend_sem,
    yrecv_sem,
    vsend_sem,
    vrecv_sem,
    msend_sem,
    mrecv_sem,
    psend_sem,
    precv_sem,
    ksend_sem,
    krecv_sem,
):
    rep = lax.axis_index("replica")
    me = lax.axis_index("dev")
    pair = lax.axis_index("pair")
    tok, half = text_ref.shape
    nvis = vision_ref.shape[0]
    shard = weight_ref.shape[0]
    own = shard // 3 // 16 * 16
    common = shard - 2 * own
    where = ring_position(me, n)

    def dev_id(d):
        return (rep, d, pair)

    other_pair = (rep, me, 1 - pair)
    other_rep = (1 - rep, me, pair)

    barrier = pltpu.get_barrier_semaphore()
    for off in range(1, n):
        pl.semaphore_signal(
            barrier, inc=1, device_id=dev_id(lax.rem(me + off, n)), device_id_type=MESH
        )
    pl.semaphore_signal(barrier, inc=1, device_id=other_pair, device_id_type=MESH)
    pl.semaphore_signal(barrier, inc=1, device_id=other_rep, device_id_type=MESH)
    local = pltpu.make_async_copy(weight_ref, wbuf.at[me], local_sem)
    local.start()
    pl.semaphore_wait(barrier, n + 1)

    def hop(buf, origin_ref, rows, way, k, send_sem, recv_sem):
        origin = ring_device(lax.rem(where - way * k + n, n), n)
        target = ring_device(lax.rem(where + way + n, n), n)
        source = buf.at[origin, rows] if k or origin_ref is None else origin_ref.at[rows]
        return pltpu.make_async_remote_copy(
            src_ref=source,
            dst_ref=buf.at[origin, rows],
            send_sem=send_sem,
            recv_sem=recv_sem,
            device_id=dev_id(target),
            device_id_type=MESH,
        )

    common_rows = pl.ds(0, common)
    own_rows = pl.ds(pl.multiple_of(common + rep * own, 16), own)
    streams = (
        (own_rows, 1, n // 2 - 1),
        (own_rows, -1, n // 2),
        (common_rows, 1, n // 2),
        (common_rows, -1, n // 2 - 1),
    )
    whops = [
        [
            hop(wbuf, weight_ref, rows, way, k, wsend_sem.at[i, k], wrecv_sem.at[i, k])
            for k in range(hops)
        ]
        for i, (rows, way, hops) in enumerate(streams)
    ]
    ycopies = []

    def ring_step(k):
        for i, (rows, way, hops) in enumerate(streams):
            if k > hops:
                continue
            if k:
                whops[i][k - 1].wait_recv()
            if k < hops:
                whops[i][k].start()
            if k and i < 2:
                origin = ring_device(lax.rem(where - way * k + n, n), n)
                index = k if way == 1 else n - k
                copy = pltpu.make_async_remote_copy(
                    src_ref=wbuf.at[origin, own_rows],
                    dst_ref=wbuf.at[origin, own_rows],
                    send_sem=ysend_sem.at[index],
                    recv_sem=yrecv_sem.at[index],
                    device_id=other_rep,
                    device_id_type=MESH,
                )
                copy.start()
                ycopies.append(copy)

    ring_step(0)

    dest_row, dest_col = dest_row_ref[...], dest_col_ref[...]
    row_i = lax.broadcasted_iota(jnp.int32, (nvis, nvis), 0)
    col_i = lax.broadcasted_iota(jnp.int32, (nvis, nvis), 1)
    same = dest_row == dest_col
    rank_col = jnp.sum(
        jnp.where(same & (col_i < row_i), 1.0, 0.0), axis=1, keepdims=True
    ).astype(jnp.int32)
    rank_row = jnp.sum(
        jnp.where(same & (row_i < col_i), 1.0, 0.0), axis=0, keepdims=True
    ).astype(jnp.int32)
    order = dest_row * cap + rank_row
    per = LANES // cap
    lane = lax.broadcasted_iota(jnp.int32, (nvis, LANES), 1)
    place = dest_col * LANES + lax.rem(me, per) * cap + rank_col
    slots = slot_col_ref[...] + 1
    for d in range(n):
        msend[d, 0:1, :] = jnp.sum(
            jnp.where(place == d * LANES + lane, slots.astype(F32), 0.0), axis=0, keepdims=True
        ).astype(jnp.int32)
        msend[d, 1:2, :] = pos_row_ref[...]
    vision = vision_ref[...]
    for block in range(n * cap // LANES):
        select = order == block * LANES + lax.broadcasted_iota(jnp.int32, (LANES, nvis), 0)
        vsend[pl.ds(block * LANES, LANES), :] = jnp.dot(
            jnp.where(select, 1.0, 0.0).astype(BF16), vision, preferred_element_type=F32
        ).astype(BF16)

    def cap_rows(d):
        return pl.ds(pl.multiple_of(d * cap, 16), cap)

    vcopies = []
    for off in range(1, n):
        target = lax.rem(me + off, n)
        for src, dst, ssem, rsem in (
            (msend.at[target], mrecv.at[me], msend_sem, mrecv_sem),
            (vsend.at[cap_rows(target)], vrecv.at[cap_rows(me)], vsend_sem, vrecv_sem),
        ):
            copy = pltpu.make_async_remote_copy(
                src_ref=src,
                dst_ref=dst,
                send_sem=ssem.at[off],
                recv_sem=rsem.at[off],
                device_id=dev_id(target),
                device_id_type=MESH,
            )
            copy.start()
            vcopies.append(copy)
    mrecv[pl.ds(me, 1)] = msend[pl.ds(me, 1)]
    vrecv[cap_rows(me), :] = vsend[cap_rows(me), :]

    ring_step(1)

    for copy in vcopies:
        copy.wait_recv()
    added = jnp.zeros((tok, half), F32)
    for g in range(n * cap // LANES):
        slot_row = sum([mrecv[s, 0:1, :] for s in range(g * per, (g + 1) * per)])
        hit = lax.broadcasted_iota(jnp.int32, (tok, LANES), 0) + 1 == slot_row
        added += jnp.dot(
            jnp.where(hit, 1.0, 0.0).astype(BF16),
            vrecv[pl.ds(g * LANES, LANES), :],
            preferred_element_type=F32,
        )
    emb[pl.ds(pair, 1)] = (text_ref[...].astype(F32) + added).astype(BF16)[None]
    pair_copy = pltpu.make_async_remote_copy(
        src_ref=emb.at[pair],
        dst_ref=emb.at[pair],
        send_sem=psend_sem,
        recv_sem=precv_sem,
        device_id=other_pair,
        device_id_type=MESH,
    )
    pair_copy.start()

    for s in range(n):
        mask[:, s * tok : (s + 1) * tok] = jnp.where(
            mrecv[s, 1:2, :] <= pos_col_ref[...], 0.0, -1e30
        )

    ring_step(2)

    pair_copy.wait_recv()
    squares = jnp.zeros((tok, 1), F32)
    for d in range(n):
        floats = emb[d // (n // 2), :, pl.ds(d % (n // 2) * shard, shard)].astype(F32)
        squares += jnp.sum(floats * floats, axis=1, keepdims=True)
    scale = lax.rsqrt(squares / (2 * half) + 1e-6)
    for d in range(n):
        floats = emb[d // (n // 2), :, pl.ds(d % (n // 2) * shard, shard)].astype(F32)
        gain = gain_ref[:, pl.ds(d * shard, shard)].astype(F32)
        nbuf[d] = (floats * scale * gain).astype(BF16)

    for k in range(3, n // 2 + 1):
        ring_step(k)
    for copy in ycopies:
        copy.wait_recv()
    local.wait()
    acc = jnp.zeros((tok, weight_ref.shape[1]), F32)
    for d in range(n):
        acc += jnp.dot(nbuf[d], wbuf[d], preferred_element_type=F32)
    kv = (acc + bias_ref[...].astype(F32)).astype(BF16)
    kvbuf[pl.ds(me, 1)] = kv[None]

    first, second = pl.ds(0, tok // 2), pl.ds(tok // 2, tok // 2)
    kstreams = (
        (first, 1, n // 2),
        (first, -1, n // 2 - 1),
        (second, 1, n // 2 - 1),
        (second, -1, n // 2),
    )
    khops = [
        [
            hop(kvbuf, None, rows, way, k, ksend_sem.at[i, k], krecv_sem.at[i, k])
            for k in range(hops)
        ]
        for i, (rows, way, hops) in enumerate(kstreams)
    ]
    for k in range(n // 2 + 1):
        for i, (rows, way, hops) in enumerate(kstreams):
            if k > hops:
                continue
            if k:
                khops[i][k - 1].wait_recv()
            if k < hops:
                khops[i][k].start()
        if k == 0:
            line = lax.broadcasted_iota(jnp.int32, (tok, tok), 1)
            pick = page_ref[...] == line
            cache_ref[...] = jnp.dot(
                jnp.where(pick, 1.0, 0.0).astype(BF16), kv, preferred_element_type=F32
            ).astype(BF16)

    heads = kv.shape[1] // (2 * HD)
    group = query_ref.shape[1] // (HD * heads)
    for head in range(heads):
        keys = kvbuf[:, :, head * 2 * HD : head * 2 * HD + HD].reshape(n * tok, HD)
        values = kvbuf[:, :, head * 2 * HD + HD : (head + 1) * 2 * HD].reshape(n * tok, HD)

        def one(j, carry, head=head, keys=keys, values=values):
            column = pl.ds(pl.multiple_of((head * group + j) * HD, HD), HD)
            scores = lax.dot_general(
                query_ref[:, column], keys, (((1,), (1,)), ((), ())), preferred_element_type=F32
            )
            scores = scores * HD ** (-0.5) + mask[...]
            peak = jnp.max(scores, axis=1, keepdims=True)
            weights = jnp.exp(scores - peak)
            total = jnp.sum(weights, axis=1, keepdims=True)
            mixed = jnp.dot(weights.astype(BF16), values, preferred_element_type=F32)
            out_ref[:, column] = (mixed / total).astype(BF16)
            return carry

        lax.fori_loop(0, group, one, 0, unroll=2 if n <= 8 else 1)

    for hops in whops + khops:
        for copy in hops:
            copy.wait_send()
    for copy in ycopies + vcopies + [pair_copy]:
        copy.wait_send()


def local(
    text_rows,
    vision_rows,
    vision_device,
    vision_slot,
    positions,
    norm_gain,
    kv_weight,
    kv_bias,
    queries,
    page_table,
):
    n = lax.axis_size("dev")
    tok, half = text_rows.shape
    nvis = vision_rows.shape[0]
    shard, columns = kv_weight.shape
    cap = max(16, 2 * nvis // n)
    pages = page_table.shape[1]
    page_rows = (
        page_table.reshape(pages, 1) * PAGE + jnp.arange(PAGE, dtype=jnp.int32)[None, :]
    ).reshape(tok, 1)
    dma = pltpu.SemaphoreType.DMA
    attended, cache = pl.pallas_call(
        functools.partial(kernel, n, cap),
        out_shape=(
            jax.ShapeDtypeStruct(queries.shape, BF16),
            jax.ShapeDtypeStruct((tok, columns), BF16),
        ),
        in_specs=[pl.BlockSpec(memory_space=pltpu.VMEM)] * 12,
        out_specs=(pl.BlockSpec(memory_space=pltpu.VMEM),) * 2,
        scratch_shapes=[
            pltpu.VMEM((n, shard, columns), BF16),
            pltpu.VMEM((n * cap, half), BF16),
            pltpu.VMEM((n * cap, half), BF16),
            pltpu.VMEM((n, 8, LANES), jnp.int32),
            pltpu.VMEM((n, 8, LANES), jnp.int32),
            pltpu.VMEM((2, tok, half), BF16),
            pltpu.VMEM((n, tok, shard), BF16),
            pltpu.VMEM((n, tok, columns), BF16),
            pltpu.VMEM((tok, n * tok), F32),
            dma,
            dma((4, n)),
            dma((4, n)),
            dma((n,)),
            dma((n,)),
            dma((n,)),
            dma((n,)),
            dma((n,)),
            dma((n,)),
            dma,
            dma,
            dma((4, n)),
            dma((4, n)),
        ],
        compiler_params=pltpu.CompilerParams(
            collective_id=0, has_side_effects=True, vmem_limit_bytes=60 * 1024 * 1024
        ),
    )(
        text_rows,
        vision_rows,
        vision_device.reshape(1, nvis),
        vision_device,
        vision_slot.reshape(nvis, 1),
        positions.reshape(1, tok),
        positions.reshape(tok, 1),
        norm_gain.reshape(1, -1),
        kv_weight,
        kv_bias.reshape(1, columns),
        queries,
        page_rows,
    )
    return (attended, cache.reshape(pages, PAGE, columns))


def solution(mesh):
    placed = (
        P(("replica", "dev"), "pair"),
        P(("replica", "dev"), "pair"),
        P(("replica", "dev"), None),
        P(("replica", "dev")),
        P(("replica", "dev")),
        P(),
        P("dev", "pair"),
        P("pair"),
        P(("replica", "dev"), "pair"),
        P(("replica", "dev"), None),
    )
    return jax.shard_map(
        local,
        mesh=mesh,
        in_specs=placed,
        out_specs=(P(("replica", "dev"), "pair"), P(("replica", "dev"), None, "pair")),
        check_vma=False,
    )
```

```python
import functools

import jax
import jax.numpy as jnp
from jax import lax
from jax.experimental import pallas as pl
from jax.experimental.pallas import tpu as pltpu
from jax.sharding import PartitionSpec as P

MESH = pl.DeviceIdType.MESH
HD = 128
PAGE = 16
LANES = 128
F32 = jnp.float32
BF16 = jnp.bfloat16


def ring_position(d, n):
    z, x = d // 2, d % 2
    return z * (1 - x) + (n - 1 - z) * x


def ring_device(r, n):
    back = r // (n // 2)
    return (1 - back) * 2 * r + back * (2 * (n - 1 - r) + 1)


def kernel(
    n,
    cap,
    text_ref,
    vision_ref,
    dest_ref,
    slot_ref,
    pos_ref,
    page_ref,
    gain_ref,
    bias_ref,
    weight_ref,
    query_ref,
    out_ref,
    cache_ref,
    wbuf,
    vsend,
    vrecv,
    msend,
    mrecv,
    emb,
    nbuf,
    kvbuf,
    mask,
    local_sem,
    wsend_sem,
    wrecv_sem,
    ysend_sem,
    yrecv_sem,
    vsend_sem,
    vrecv_sem,
    msend_sem,
    mrecv_sem,
    psend_sem,
    precv_sem,
    ksend_sem,
    krecv_sem,
):
    rep = lax.axis_index("replica")
    me = lax.axis_index("dev")
    pair = lax.axis_index("pair")
    tok, half = text_ref.shape
    nvis = vision_ref.shape[0]
    shard = weight_ref.shape[0]
    own = shard * 2 // 5 // 16 * 16
    common = shard - 2 * own
    where = ring_position(me, n)

    def dev_id(d):
        return (rep, d, pair)

    other_pair = (rep, me, 1 - pair)
    other_rep = (1 - rep, me, pair)

    barrier = pltpu.get_barrier_semaphore()
    for off in range(1, n):
        pl.semaphore_signal(
            barrier, inc=1, device_id=dev_id(lax.rem(me + off, n)), device_id_type=MESH
        )
    pl.semaphore_signal(barrier, inc=1, device_id=other_pair, device_id_type=MESH)
    pl.semaphore_signal(barrier, inc=1, device_id=other_rep, device_id_type=MESH)
    local = pltpu.make_async_copy(weight_ref, wbuf.at[me], local_sem)
    local.start()
    pl.semaphore_wait(barrier, n + 1)

    def hop(buf, origin_ref, rows, way, k, send_sem, recv_sem):
        origin = ring_device(lax.rem(where - way * k + n, n), n)
        target = ring_device(lax.rem(where + way + n, n), n)
        source = buf.at[origin, rows] if k or origin_ref is None else origin_ref.at[rows]
        return pltpu.make_async_remote_copy(
            src_ref=source,
            dst_ref=buf.at[origin, rows],
            send_sem=send_sem,
            recv_sem=recv_sem,
            device_id=dev_id(target),
            device_id_type=MESH,
        )

    own_at = common + rep * own
    own_cut = (own // 2 + 15) // 16 * 16
    common_cut = (common // 2 + 15) // 16 * 16
    own_parts = (
        pl.ds(pl.multiple_of(own_at, 16), own_cut),
        pl.ds(pl.multiple_of(own_at + own_cut, 16), own - own_cut),
    )
    common_parts = (pl.ds(0, common_cut), pl.ds(common_cut, common - common_cut))
    far = n // 2
    streams = (
        (own_parts[0], 1, far - 1),
        (own_parts[1], -1, far - 1),
        (own_parts[1], 1, far),
        (own_parts[0], -1, far),
        (common_parts[0], 1, far),
        (common_parts[1], -1, far),
        (common_parts[1], 1, far - 1),
        (common_parts[0], -1, far - 1),
    )
    whops = [
        [
            hop(wbuf, weight_ref, rows, way, k, wsend_sem.at[i, k], wrecv_sem.at[i, k])
            for k in range(hops)
        ]
        for i, (rows, way, hops) in enumerate(streams)
    ]
    ycopies = {}

    def ring_step(k):
        for i, (rows, way, hops) in enumerate(streams):
            if k > hops:
                continue
            if k:
                whops[i][k - 1].wait_recv()
            if k < hops:
                whops[i][k].start()
            if k and i < 4:
                origin = ring_device(lax.rem(where - way * k + n, n), n)
                index = k if way == 1 else n - k
                part = (0, 1, 1, 0)[i]
                copy = pltpu.make_async_remote_copy(
                    src_ref=wbuf.at[origin, rows],
                    dst_ref=wbuf.at[origin, rows],
                    send_sem=ysend_sem.at[part, index],
                    recv_sem=yrecv_sem.at[part, index],
                    device_id=other_rep,
                    device_id_type=MESH,
                )
                copy.start()
                ycopies[part, index] = copy

    ring_step(0)

    def column(line, size):
        diagonal = lax.broadcasted_iota(jnp.int32, (size, size), 0) == lax.broadcasted_iota(
            jnp.int32, (size, size), 1
        )
        return jnp.sum(
            jnp.where(diagonal, line.astype(F32), 0.0), axis=1, keepdims=True
        ).astype(jnp.int32)

    dest_row = dest_ref[...]
    dest_col = column(dest_row, nvis)
    pos_row = pos_ref[...]
    pos_col = column(pos_row, tok)
    pages = page_ref.shape[1]
    row_of = lax.broadcasted_iota(jnp.int32, (tok, pages), 0)
    page_of = lax.broadcasted_iota(jnp.int32, (tok, pages), 1)
    first_row = page_of * PAGE
    in_page = (row_of >= first_row) & (row_of < first_row + PAGE)
    page_col = jnp.sum(
        jnp.where(in_page, (page_ref[...] * PAGE + row_of - first_row).astype(F32), 0.0),
        axis=1,
        keepdims=True,
    ).astype(jnp.int32)
    row_i = lax.broadcasted_iota(jnp.int32, (nvis, nvis), 0)
    col_i = lax.broadcasted_iota(jnp.int32, (nvis, nvis), 1)
    same = dest_row == dest_col
    rank_col = jnp.sum(
        jnp.where(same & (col_i < row_i), 1.0, 0.0), axis=1, keepdims=True
    ).astype(jnp.int32)
    rank_row = jnp.sum(
        jnp.where(same & (row_i < col_i), 1.0, 0.0), axis=0, keepdims=True
    ).astype(jnp.int32)
    order = dest_row * cap + rank_row
    per = LANES // cap
    lane = lax.broadcasted_iota(jnp.int32, (nvis, LANES), 1)
    place = dest_col * LANES + lax.rem(me, per) * cap + rank_col
    slots = column(slot_ref[...], nvis) + 1
    for d in range(n):
        msend[d, 0:1, :] = jnp.sum(
            jnp.where(place == d * LANES + lane, slots.astype(F32), 0.0), axis=0, keepdims=True
        ).astype(jnp.int32)
        msend[d, 1:2, :] = pos_row
    vision = vision_ref[...]
    for block in range(n * cap // LANES):
        select = order == block * LANES + lax.broadcasted_iota(jnp.int32, (LANES, nvis), 0)
        vsend[pl.ds(block * LANES, LANES), :] = jnp.dot(
            jnp.where(select, 1.0, 0.0).astype(BF16), vision, preferred_element_type=F32
        ).astype(BF16)

    def cap_rows(d):
        return pl.ds(pl.multiple_of(d * cap, 16), cap)

    vcopies = []
    for off in range(1, n):
        target = lax.rem(me + off, n)
        for src, dst, ssem, rsem in (
            (msend.at[target], mrecv.at[me], msend_sem, mrecv_sem),
            (vsend.at[cap_rows(target)], vrecv.at[cap_rows(me)], vsend_sem, vrecv_sem),
        ):
            copy = pltpu.make_async_remote_copy(
                src_ref=src,
                dst_ref=dst,
                send_sem=ssem.at[off],
                recv_sem=rsem.at[off],
                device_id=dev_id(target),
                device_id_type=MESH,
            )
            copy.start()
            vcopies.append(copy)
    mrecv[pl.ds(me, 1)] = msend[pl.ds(me, 1)]
    vrecv[cap_rows(me), :] = vsend[cap_rows(me), :]

    ring_step(1)
    for k in range(2, far - 1):
        ring_step(k)

    for copy in vcopies:
        copy.wait_recv()
    added = jnp.zeros((tok, half), F32)
    for g in range(n * cap // LANES):
        slot_row = sum([mrecv[s, 0:1, :] for s in range(g * per, (g + 1) * per)])
        hit = lax.broadcasted_iota(jnp.int32, (tok, LANES), 0) + 1 == slot_row
        added += jnp.dot(
            jnp.where(hit, 1.0, 0.0).astype(BF16),
            vrecv[pl.ds(g * LANES, LANES), :],
            preferred_element_type=F32,
        )
    emb[pl.ds(pair, 1)] = (text_ref[...].astype(F32) + added).astype(BF16)[None]
    pair_copy = pltpu.make_async_remote_copy(
        src_ref=emb.at[pair],
        dst_ref=emb.at[pair],
        send_sem=psend_sem,
        recv_sem=precv_sem,
        device_id=other_pair,
        device_id_type=MESH,
    )
    pair_copy.start()

    for s in range(n):
        mask[:, s * tok : (s + 1) * tok] = jnp.where(
            mrecv[s, 1:2, :] <= pos_col, 0.0, -1e30
        )

    ring_step(far - 1)

    pair_copy.wait_recv()
    squares = jnp.zeros((tok, 1), F32)
    for d in range(n):
        floats = emb[d // (n // 2), :, pl.ds(d % (n // 2) * shard, shard)].astype(F32)
        squares += jnp.sum(floats * floats, axis=1, keepdims=True)
    scale = lax.rsqrt(squares / (2 * half) + 1e-6)
    for d in range(n):
        floats = emb[d // (n // 2), :, pl.ds(d % (n // 2) * shard, shard)].astype(F32)
        gain = gain_ref[:, pl.ds(d * shard, shard)].astype(F32)
        nbuf[d] = (floats * scale * gain).astype(BF16)

    local.wait()
    acc = jnp.dot(nbuf[me], wbuf[me], preferred_element_type=F32)

    def projected(total, steps):
        for step in steps:
            for part in range(2):
                ycopies[part, step].wait_recv()
            d = ring_device(lax.rem(where - step + n, n), n)
            total += jnp.dot(nbuf[d], wbuf[d], preferred_element_type=F32)
        return total

    near = [k for step in range(1, far - 1) for k in (step, n - step)]
    acc = projected(acc, near)
    ring_step(far)
    acc = projected(acc, (far - 1, far + 1, far))
    kv = (acc + bias_ref[...].astype(F32)).astype(BF16)
    kvbuf[pl.ds(me, 1)] = kv[None]

    first, second = pl.ds(0, tok // 2), pl.ds(tok // 2, tok // 2)
    kstreams = (
        (first, 1, n // 2),
        (first, -1, n // 2 - 1),
        (second, 1, n // 2 - 1),
        (second, -1, n // 2),
    )
    khops = [
        [
            hop(kvbuf, None, rows, way, k, ksend_sem.at[i, k], krecv_sem.at[i, k])
            for k in range(hops)
        ]
        for i, (rows, way, hops) in enumerate(kstreams)
    ]
    for k in range(n // 2 + 1):
        for i, (rows, way, hops) in enumerate(kstreams):
            if k > hops:
                continue
            if k:
                khops[i][k - 1].wait_recv()
            if k < hops:
                khops[i][k].start()
        if k == 0:
            line = lax.broadcasted_iota(jnp.int32, (tok, tok), 1)
            pick = page_col == line
            cache_ref[...] = jnp.dot(
                jnp.where(pick, 1.0, 0.0).astype(BF16), kv, preferred_element_type=F32
            ).astype(BF16)

    heads = kv.shape[1] // (2 * HD)
    group = query_ref.shape[1] // (HD * heads)
    for head in range(heads):
        keys = kvbuf[:, :, head * 2 * HD : head * 2 * HD + HD].reshape(n * tok, HD)
        values = kvbuf[:, :, head * 2 * HD + HD : (head + 1) * 2 * HD].reshape(n * tok, HD)

        def one(j, carry, head=head, keys=keys, values=values):
            span = pl.ds(pl.multiple_of((head * group + j) * HD, HD), HD)
            scores = lax.dot_general(
                query_ref[:, span], keys, (((1,), (1,)), ((), ())), preferred_element_type=F32
            )
            scores = scores * HD ** (-0.5) + mask[...]
            peak = jnp.max(scores, axis=1, keepdims=True)
            weights = jnp.exp(scores - peak)
            total = jnp.sum(weights, axis=1, keepdims=True)
            mixed = jnp.dot(weights.astype(BF16), values, preferred_element_type=F32)
            out_ref[:, span] = (mixed / total).astype(BF16)
            return carry

        lax.fori_loop(0, group, one, 0, unroll=2 if n <= 8 else 1)

    for hops in whops + khops:
        for copy in hops:
            copy.wait_send()
    for copy in list(ycopies.values()) + vcopies + [pair_copy]:
        copy.wait_send()


def local(
    text_rows,
    vision_rows,
    vision_device,
    vision_slot,
    positions,
    norm_gain,
    kv_weight,
    kv_bias,
    queries,
    page_table,
):
    n = lax.axis_size("dev")
    tok, half = text_rows.shape
    nvis = vision_rows.shape[0]
    shard, columns = kv_weight.shape
    cap = max(16, 2 * nvis // n)
    pages = page_table.shape[1]
    dma = pltpu.SemaphoreType.DMA
    attended, cache = pl.pallas_call(
        functools.partial(kernel, n, cap),
        out_shape=(
            jax.ShapeDtypeStruct(queries.shape, BF16),
            jax.ShapeDtypeStruct((tok, columns), BF16),
        ),
        in_specs=[pl.BlockSpec(memory_space=pltpu.VMEM)] * 10,
        out_specs=(pl.BlockSpec(memory_space=pltpu.VMEM),) * 2,
        scratch_shapes=[
            pltpu.VMEM((n, shard, columns), BF16),
            pltpu.VMEM((n * cap, half), BF16),
            pltpu.VMEM((n * cap, half), BF16),
            pltpu.VMEM((n, 8, LANES), jnp.int32),
            pltpu.VMEM((n, 8, LANES), jnp.int32),
            pltpu.VMEM((2, tok, half), BF16),
            pltpu.VMEM((n, tok, shard), BF16),
            pltpu.VMEM((n, tok, columns), BF16),
            pltpu.VMEM((tok, n * tok), F32),
            dma,
            dma((8, n)),
            dma((8, n)),
            dma((2, n)),
            dma((2, n)),
            dma((n,)),
            dma((n,)),
            dma((n,)),
            dma((n,)),
            dma,
            dma,
            dma((4, n)),
            dma((4, n)),
        ],
        compiler_params=pltpu.CompilerParams(
            collective_id=0, has_side_effects=True, vmem_limit_bytes=60 * 1024 * 1024
        ),
    )(
        text_rows,
        vision_rows,
        vision_device.reshape(1, nvis),
        vision_slot.reshape(1, nvis),
        positions.reshape(1, tok),
        page_table,
        norm_gain.reshape(1, -1),
        kv_bias.reshape(1, -1),
        kv_weight,
        queries,
    )
    return (attended, cache.reshape(pages, PAGE, columns))


def solution(mesh):
    placed = (
        P(("replica", "dev"), "pair"),
        P(("replica", "dev"), "pair"),
        P(("replica", "dev"), None),
        P(("replica", "dev")),
        P(("replica", "dev")),
        P(),
        P("dev", "pair"),
        P("pair"),
        P(("replica", "dev"), "pair"),
        P(("replica", "dev"), None),
    )
    return jax.shard_map(
        local,
        mesh=mesh,
        in_specs=placed,
        out_specs=(P(("replica", "dev"), "pair"), P(("replica", "dev"), None, "pair")),
        check_vma=False,
    )
```

```python
import functools

import jax
import jax.numpy as jnp
from jax import lax
from jax.experimental import pallas as pl
from jax.experimental.pallas import tpu as pltpu
from jax.sharding import PartitionSpec as P

MESH = pl.DeviceIdType.MESH
HD = 128
PAGE = 16
LANES = 128
F32 = jnp.float32
BF16 = jnp.bfloat16


def ring_position(d, n):
    z, x = d // 2, d % 2
    return z * (1 - x) + (n - 1 - z) * x


def ring_device(r, n):
    back = r // (n // 2)
    return (1 - back) * 2 * r + back * (2 * (n - 1 - r) + 1)


def kernel(
    n,
    cap,
    text_ref,
    vision_ref,
    dest_ref,
    slot_ref,
    pos_ref,
    page_ref,
    gain_ref,
    bias_ref,
    weight_ref,
    query_ref,
    out_ref,
    cache_ref,
    wbuf,
    vsend,
    vrecv,
    msend,
    mrecv,
    emb,
    nbuf,
    kvbuf,
    mask,
    local_sem,
    wsend_sem,
    wrecv_sem,
    ysend_sem,
    yrecv_sem,
    vsend_sem,
    vrecv_sem,
    msend_sem,
    mrecv_sem,
    psend_sem,
    precv_sem,
    ksend_sem,
    krecv_sem,
):
    rep = lax.axis_index("replica")
    me = lax.axis_index("dev")
    pair = lax.axis_index("pair")
    tok, half = text_ref.shape
    nvis = vision_ref.shape[0]
    shard = weight_ref.shape[0]
    own = shard // 3 // 16 * 16
    common = shard - 2 * own
    where = ring_position(me, n)

    def dev_id(d):
        return (rep, d, pair)

    other_pair = (rep, me, 1 - pair)
    other_rep = (1 - rep, me, pair)

    barrier = pltpu.get_barrier_semaphore()
    for off in range(1, n):
        pl.semaphore_signal(
            barrier, inc=1, device_id=dev_id(lax.rem(me + off, n)), device_id_type=MESH
        )
    pl.semaphore_signal(barrier, inc=1, device_id=other_pair, device_id_type=MESH)
    pl.semaphore_signal(barrier, inc=1, device_id=other_rep, device_id_type=MESH)
    local = pltpu.make_async_copy(weight_ref, wbuf.at[me], local_sem)
    local.start()
    pl.semaphore_wait(barrier, n + 1)

    def hop(buf, origin_ref, rows, way, k, send_sem, recv_sem):
        origin = ring_device(lax.rem(where - way * k + n, n), n)
        target = ring_device(lax.rem(where + way + n, n), n)
        source = buf.at[origin, rows] if k or origin_ref is None else origin_ref.at[rows]
        return pltpu.make_async_remote_copy(
            src_ref=source,
            dst_ref=buf.at[origin, rows],
            send_sem=send_sem,
            recv_sem=recv_sem,
            device_id=dev_id(target),
            device_id_type=MESH,
        )

    own_at = common + rep * own
    own_cut = (own // 2 + 15) // 16 * 16
    common_cut = (common // 2 + 15) // 16 * 16
    own_parts = (
        pl.ds(pl.multiple_of(own_at, 16), own_cut),
        pl.ds(pl.multiple_of(own_at + own_cut, 16), own - own_cut),
    )
    common_parts = (pl.ds(0, common_cut), pl.ds(common_cut, common - common_cut))
    far = n // 2
    streams = (
        (own_parts[0], 1, far - 1),
        (own_parts[1], -1, far - 1),
        (own_parts[1], 1, far),
        (own_parts[0], -1, far),
        (common_parts[0], 1, far),
        (common_parts[1], -1, far),
        (common_parts[1], 1, far - 1),
        (common_parts[0], -1, far - 1),
    )
    whops = [
        [
            hop(wbuf, weight_ref, rows, way, k, wsend_sem.at[i, k], wrecv_sem.at[i, k])
            for k in range(hops)
        ]
        for i, (rows, way, hops) in enumerate(streams)
    ]
    ycopies = {}

    def ring_step(k):
        for i, (rows, way, hops) in enumerate(streams):
            if k > hops:
                continue
            if k:
                whops[i][k - 1].wait_recv()
            if k < hops:
                whops[i][k].start()
            if k and i < 4:
                origin = ring_device(lax.rem(where - way * k + n, n), n)
                index = k if way == 1 else n - k
                part = (0, 1, 1, 0)[i]
                copy = pltpu.make_async_remote_copy(
                    src_ref=wbuf.at[origin, rows],
                    dst_ref=wbuf.at[origin, rows],
                    send_sem=ysend_sem.at[part, index],
                    recv_sem=yrecv_sem.at[part, index],
                    device_id=other_rep,
                    device_id_type=MESH,
                )
                copy.start()
                ycopies[part, index] = copy

    ring_step(0)

    def column(line, size):
        diagonal = lax.broadcasted_iota(jnp.int32, (size, size), 0) == lax.broadcasted_iota(
            jnp.int32, (size, size), 1
        )
        return jnp.sum(
            jnp.where(diagonal, line.astype(F32), 0.0), axis=1, keepdims=True
        ).astype(jnp.int32)

    dest_row = dest_ref[...]
    dest_col = column(dest_row, nvis)
    pos_row = pos_ref[...]
    pos_col = column(pos_row, tok)
    pages = page_ref.shape[1]
    row_of = lax.broadcasted_iota(jnp.int32, (tok, pages), 0)
    page_of = lax.broadcasted_iota(jnp.int32, (tok, pages), 1)
    first_row = page_of * PAGE
    in_page = (row_of >= first_row) & (row_of < first_row + PAGE)
    page_col = jnp.sum(
        jnp.where(in_page, (page_ref[...] * PAGE + row_of - first_row).astype(F32), 0.0),
        axis=1,
        keepdims=True,
    ).astype(jnp.int32)
    row_i = lax.broadcasted_iota(jnp.int32, (nvis, nvis), 0)
    col_i = lax.broadcasted_iota(jnp.int32, (nvis, nvis), 1)
    same = dest_row == dest_col
    rank_col = jnp.sum(
        jnp.where(same & (col_i < row_i), 1.0, 0.0), axis=1, keepdims=True
    ).astype(jnp.int32)
    rank_row = jnp.sum(
        jnp.where(same & (row_i < col_i), 1.0, 0.0), axis=0, keepdims=True
    ).astype(jnp.int32)
    order = dest_row * cap + rank_row
    per = LANES // cap
    lane = lax.broadcasted_iota(jnp.int32, (nvis, LANES), 1)
    place = dest_col * LANES + lax.rem(me, per) * cap + rank_col
    slots = column(slot_ref[...], nvis) + 1
    for d in range(n):
        msend[d, 0:1, :] = jnp.sum(
            jnp.where(place == d * LANES + lane, slots.astype(F32), 0.0), axis=0, keepdims=True
        ).astype(jnp.int32)
        msend[d, 1:2, :] = pos_row
    vision = vision_ref[...]
    for block in range(n * cap // LANES):
        select = order == block * LANES + lax.broadcasted_iota(jnp.int32, (LANES, nvis), 0)
        vsend[pl.ds(block * LANES, LANES), :] = jnp.dot(
            jnp.where(select, 1.0, 0.0).astype(BF16), vision, preferred_element_type=F32
        ).astype(BF16)

    def cap_rows(d):
        return pl.ds(pl.multiple_of(d * cap, 16), cap)

    vcopies = []
    for off in range(1, n):
        target = lax.rem(me + off, n)
        for src, dst, ssem, rsem in (
            (msend.at[target], mrecv.at[me], msend_sem, mrecv_sem),
            (vsend.at[cap_rows(target)], vrecv.at[cap_rows(me)], vsend_sem, vrecv_sem),
        ):
            copy = pltpu.make_async_remote_copy(
                src_ref=src,
                dst_ref=dst,
                send_sem=ssem.at[off],
                recv_sem=rsem.at[off],
                device_id=dev_id(target),
                device_id_type=MESH,
            )
            copy.start()
            vcopies.append(copy)
    mrecv[pl.ds(me, 1)] = msend[pl.ds(me, 1)]
    vrecv[cap_rows(me), :] = vsend[cap_rows(me), :]

    ring_step(1)
    for k in range(2, far - 1):
        ring_step(k)

    for copy in vcopies:
        copy.wait_recv()
    added = jnp.zeros((tok, half), F32)
    for g in range(n * cap // LANES):
        slot_row = sum([mrecv[s, 0:1, :] for s in range(g * per, (g + 1) * per)])
        hit = lax.broadcasted_iota(jnp.int32, (tok, LANES), 0) + 1 == slot_row
        added += jnp.dot(
            jnp.where(hit, 1.0, 0.0).astype(BF16),
            vrecv[pl.ds(g * LANES, LANES), :],
            preferred_element_type=F32,
        )
    emb[pl.ds(pair, 1)] = (text_ref[...].astype(F32) + added).astype(BF16)[None]
    pair_copy = pltpu.make_async_remote_copy(
        src_ref=emb.at[pair],
        dst_ref=emb.at[pair],
        send_sem=psend_sem,
        recv_sem=precv_sem,
        device_id=other_pair,
        device_id_type=MESH,
    )
    pair_copy.start()

    for s in range(n):
        mask[:, s * tok : (s + 1) * tok] = jnp.where(
            mrecv[s, 1:2, :] <= pos_col, 0.0, -1e30
        )

    ring_step(far - 1)

    pair_copy.wait_recv()
    squares = jnp.zeros((tok, 1), F32)
    for d in range(n):
        floats = emb[d // (n // 2), :, pl.ds(d % (n // 2) * shard, shard)].astype(F32)
        squares += jnp.sum(floats * floats, axis=1, keepdims=True)
    scale = lax.rsqrt(squares / (2 * half) + 1e-6)
    for d in range(n):
        floats = emb[d // (n // 2), :, pl.ds(d % (n // 2) * shard, shard)].astype(F32)
        gain = gain_ref[:, pl.ds(d * shard, shard)].astype(F32)
        nbuf[d] = (floats * scale * gain).astype(BF16)

    local.wait()
    acc = jnp.dot(nbuf[me], wbuf[me], preferred_element_type=F32)

    def projected(total, steps):
        for step in steps:
            for part in range(2):
                ycopies[part, step].wait_recv()
            d = ring_device(lax.rem(where - step + n, n), n)
            total += jnp.dot(nbuf[d], wbuf[d], preferred_element_type=F32)
        return total

    near = [k for step in range(1, far - 1) for k in (step, n - step)]
    acc = projected(acc, near)
    ring_step(far)
    acc = projected(acc, (far - 1, far + 1, far))
    kv = (acc + bias_ref[...].astype(F32)).astype(BF16)
    kvbuf[pl.ds(me, 1)] = kv[None]

    first, second = pl.ds(0, tok // 2), pl.ds(tok // 2, tok // 2)
    kstreams = (
        (first, 1, n // 2),
        (first, -1, n // 2 - 1),
        (second, 1, n // 2 - 1),
        (second, -1, n // 2),
    )
    khops = [
        [
            hop(kvbuf, None, rows, way, k, ksend_sem.at[i, k], krecv_sem.at[i, k])
            for k in range(hops)
        ]
        for i, (rows, way, hops) in enumerate(kstreams)
    ]
    for k in range(n // 2 + 1):
        for i, (rows, way, hops) in enumerate(kstreams):
            if k > hops:
                continue
            if k:
                khops[i][k - 1].wait_recv()
            if k < hops:
                khops[i][k].start()
        if k == 0:
            line = lax.broadcasted_iota(jnp.int32, (tok, tok), 1)
            pick = page_col == line
            cache_ref[...] = jnp.dot(
                jnp.where(pick, 1.0, 0.0).astype(BF16), kv, preferred_element_type=F32
            ).astype(BF16)

    heads = kv.shape[1] // (2 * HD)
    group = query_ref.shape[1] // (HD * heads)
    for head in range(heads):
        keys = kvbuf[:, :, head * 2 * HD : head * 2 * HD + HD].reshape(n * tok, HD)
        values = kvbuf[:, :, head * 2 * HD + HD : (head + 1) * 2 * HD].reshape(n * tok, HD)

        def one(j, carry, head=head, keys=keys, values=values):
            span = pl.ds(pl.multiple_of((head * group + j) * HD, HD), HD)
            scores = lax.dot_general(
                query_ref[:, span], keys, (((1,), (1,)), ((), ())), preferred_element_type=F32
            )
            scores = scores * HD ** (-0.5) + mask[...]
            peak = jnp.max(scores, axis=1, keepdims=True)
            weights = jnp.exp(scores - peak)
            total = jnp.sum(weights, axis=1, keepdims=True)
            mixed = jnp.dot(weights.astype(BF16), values, preferred_element_type=F32)
            out_ref[:, span] = (mixed / total).astype(BF16)
            return carry

        lax.fori_loop(0, group, one, 0, unroll=2 if n <= 8 else 1)

    for hops in whops + khops:
        for copy in hops:
            copy.wait_send()
    for copy in list(ycopies.values()) + vcopies + [pair_copy]:
        copy.wait_send()


def local(
    text_rows,
    vision_rows,
    vision_device,
    vision_slot,
    positions,
    norm_gain,
    kv_weight,
    kv_bias,
    queries,
    page_table,
):
    n = lax.axis_size("dev")
    tok, half = text_rows.shape
    nvis = vision_rows.shape[0]
    shard, columns = kv_weight.shape
    cap = max(16, 2 * nvis // n)
    pages = page_table.shape[1]
    dma = pltpu.SemaphoreType.DMA
    attended, cache = pl.pallas_call(
        functools.partial(kernel, n, cap),
        out_shape=(
            jax.ShapeDtypeStruct(queries.shape, BF16),
            jax.ShapeDtypeStruct((tok, columns), BF16),
        ),
        in_specs=[pl.BlockSpec(memory_space=pltpu.VMEM)] * 10,
        out_specs=(pl.BlockSpec(memory_space=pltpu.VMEM),) * 2,
        scratch_shapes=[
            pltpu.VMEM((n, shard, columns), BF16),
            pltpu.VMEM((n * cap, half), BF16),
            pltpu.VMEM((n * cap, half), BF16),
            pltpu.VMEM((n, 8, LANES), jnp.int32),
            pltpu.VMEM((n, 8, LANES), jnp.int32),
            pltpu.VMEM((2, tok, half), BF16),
            pltpu.VMEM((n, tok, shard), BF16),
            pltpu.VMEM((n, tok, columns), BF16),
            pltpu.VMEM((tok, n * tok), F32),
            dma,
            dma((8, n)),
            dma((8, n)),
            dma((2, n)),
            dma((2, n)),
            dma((n,)),
            dma((n,)),
            dma((n,)),
            dma((n,)),
            dma,
            dma,
            dma((4, n)),
            dma((4, n)),
        ],
        compiler_params=pltpu.CompilerParams(
            collective_id=0, has_side_effects=True, vmem_limit_bytes=60 * 1024 * 1024
        ),
    )(
        text_rows,
        vision_rows,
        vision_device.reshape(1, nvis),
        vision_slot.reshape(1, nvis),
        positions.reshape(1, tok),
        page_table,
        norm_gain.reshape(1, -1),
        kv_bias.reshape(1, -1),
        kv_weight,
        queries,
    )
    return (attended, cache.reshape(pages, PAGE, columns))


def solution(mesh):
    placed = (
        P(("replica", "dev"), "pair"),
        P(("replica", "dev"), "pair"),
        P(("replica", "dev"), None),
        P(("replica", "dev")),
        P(("replica", "dev")),
        P(),
        P("dev", "pair"),
        P("pair"),
        P(("replica", "dev"), "pair"),
        P(("replica", "dev"), None),
    )
    return jax.shard_map(
        local,
        mesh=mesh,
        in_specs=placed,
        out_specs=(P(("replica", "dev"), "pair"), P(("replica", "dev"), None, "pair")),
        check_vma=False,
    )
```

```python
import functools

import jax
import jax.numpy as jnp
from jax import lax
from jax.experimental import pallas as pl
from jax.experimental.pallas import tpu as pltpu
from jax.sharding import PartitionSpec as P

MESH = pl.DeviceIdType.MESH
HD = 128
PAGE = 16
LANES = 128
F32 = jnp.float32
BF16 = jnp.bfloat16


def ring_position(d, n):
    z, x = d // 2, d % 2
    return z * (1 - x) + (n - 1 - z) * x


def ring_device(r, n):
    back = r // (n // 2)
    return (1 - back) * 2 * r + back * (2 * (n - 1 - r) + 1)


def kernel(
    n,
    cap,
    text_ref,
    vision_ref,
    dest_ref,
    slot_ref,
    pos_ref,
    page_ref,
    gain_ref,
    bias_ref,
    weight_ref,
    query_ref,
    out_ref,
    cache_ref,
    wbuf,
    vsend,
    vrecv,
    msend,
    mrecv,
    emb,
    nbuf,
    kvbuf,
    mask,
    local_sem,
    wsend_sem,
    wrecv_sem,
    ysend_sem,
    yrecv_sem,
    vsend_sem,
    vrecv_sem,
    msend_sem,
    mrecv_sem,
    psend_sem,
    precv_sem,
    ksend_sem,
    krecv_sem,
):
    rep = lax.axis_index("replica")
    me = lax.axis_index("dev")
    pair = lax.axis_index("pair")
    tok, half = text_ref.shape
    nvis = vision_ref.shape[0]
    shard = weight_ref.shape[0]
    own = shard // 3 // 16 * 16
    common = shard - 2 * own
    where = ring_position(me, n)

    def dev_id(d):
        return (rep, d, pair)

    other_pair = (rep, me, 1 - pair)
    other_rep = (1 - rep, me, pair)

    barrier = pltpu.get_barrier_semaphore()
    for off in range(1, n):
        pl.semaphore_signal(
            barrier, inc=1, device_id=dev_id(lax.rem(me + off, n)), device_id_type=MESH
        )
    pl.semaphore_signal(barrier, inc=1, device_id=other_pair, device_id_type=MESH)
    pl.semaphore_signal(barrier, inc=1, device_id=other_rep, device_id_type=MESH)
    local = pltpu.make_async_copy(weight_ref, wbuf.at[me], local_sem)
    local.start()
    pl.semaphore_wait(barrier, n + 1)

    def hop(buf, origin_ref, rows, way, k, send_sem, recv_sem):
        origin = ring_device(lax.rem(where - way * k + n, n), n)
        target = ring_device(lax.rem(where + way + n, n), n)
        source = buf.at[origin, rows] if k or origin_ref is None else origin_ref.at[rows]
        return pltpu.make_async_remote_copy(
            src_ref=source,
            dst_ref=buf.at[origin, rows],
            send_sem=send_sem,
            recv_sem=recv_sem,
            device_id=dev_id(target),
            device_id_type=MESH,
        )

    own_at = common + rep * own
    own_cut = (own // 2 + 15) // 16 * 16
    common_cut = (common // 2 + 15) // 16 * 16
    own_parts = (
        pl.ds(pl.multiple_of(own_at, 16), own_cut),
        pl.ds(pl.multiple_of(own_at + own_cut, 16), own - own_cut),
    )
    common_parts = (pl.ds(0, common_cut), pl.ds(common_cut, common - common_cut))
    far = n // 2
    streams = (
        (own_parts[0], 1, far - 1),
        (own_parts[1], -1, far - 1),
        (own_parts[1], 1, far),
        (own_parts[0], -1, far),
        (common_parts[0], 1, far),
        (common_parts[1], -1, far),
        (common_parts[1], 1, far - 1),
        (common_parts[0], -1, far - 1),
    )
    whops = [
        [
            hop(wbuf, weight_ref, rows, way, k, wsend_sem.at[i, k], wrecv_sem.at[i, k])
            for k in range(hops)
        ]
        for i, (rows, way, hops) in enumerate(streams)
    ]
    ycopies = {}

    def ring_step(k):
        for i, (rows, way, hops) in enumerate(streams):
            if k > hops:
                continue
            if k:
                whops[i][k - 1].wait_recv()
            if k < hops:
                whops[i][k].start()
            if k and i < 4:
                origin = ring_device(lax.rem(where - way * k + n, n), n)
                index = k if way == 1 else n - k
                part = (0, 1, 1, 0)[i]
                copy = pltpu.make_async_remote_copy(
                    src_ref=wbuf.at[origin, rows],
                    dst_ref=wbuf.at[origin, rows],
                    send_sem=ysend_sem.at[part, index],
                    recv_sem=yrecv_sem.at[part, index],
                    device_id=other_rep,
                    device_id_type=MESH,
                )
                copy.start()
                ycopies[part, index] = copy

    ring_step(0)

    def column(line, size):
        diagonal = lax.broadcasted_iota(jnp.int32, (size, size), 0) == lax.broadcasted_iota(
            jnp.int32, (size, size), 1
        )
        return jnp.sum(
            jnp.where(diagonal, line.astype(F32), 0.0), axis=1, keepdims=True
        ).astype(jnp.int32)

    dest_row = dest_ref[...]
    dest_col = column(dest_row, nvis)
    pos_row = pos_ref[...]
    pos_col = column(pos_row, tok)
    pages = page_ref.shape[1]
    row_of = lax.broadcasted_iota(jnp.int32, (tok, pages), 0)
    page_of = lax.broadcasted_iota(jnp.int32, (tok, pages), 1)
    first_row = page_of * PAGE
    in_page = (row_of >= first_row) & (row_of < first_row + PAGE)
    page_col = jnp.sum(
        jnp.where(in_page, (page_ref[...] * PAGE + row_of - first_row).astype(F32), 0.0),
        axis=1,
        keepdims=True,
    ).astype(jnp.int32)
    row_i = lax.broadcasted_iota(jnp.int32, (nvis, nvis), 0)
    col_i = lax.broadcasted_iota(jnp.int32, (nvis, nvis), 1)
    same = dest_row == dest_col
    rank_col = jnp.sum(
        jnp.where(same & (col_i < row_i), 1.0, 0.0), axis=1, keepdims=True
    ).astype(jnp.int32)
    rank_row = jnp.sum(
        jnp.where(same & (row_i < col_i), 1.0, 0.0), axis=0, keepdims=True
    ).astype(jnp.int32)
    order = dest_row * cap + rank_row
    per = LANES // cap
    lane = lax.broadcasted_iota(jnp.int32, (nvis, LANES), 1)
    place = dest_col * LANES + lax.rem(me, per) * cap + rank_col
    slots = column(slot_ref[...], nvis) + 1
    for d in range(n):
        msend[d, 0:1, :] = jnp.sum(
            jnp.where(place == d * LANES + lane, slots.astype(F32), 0.0), axis=0, keepdims=True
        ).astype(jnp.int32)
        msend[d, 1:2, :] = pos_row
    vision = vision_ref[...]
    for block in range(n * cap // LANES):
        select = order == block * LANES + lax.broadcasted_iota(jnp.int32, (LANES, nvis), 0)
        vsend[pl.ds(block * LANES, LANES), :] = jnp.dot(
            jnp.where(select, 1.0, 0.0).astype(BF16), vision, preferred_element_type=F32
        ).astype(BF16)

    def cap_rows(d):
        return pl.ds(pl.multiple_of(d * cap, 16), cap)

    vcopies = []
    for off in range(1, n):
        target = lax.rem(me + off, n)
        for src, dst, ssem, rsem in (
            (msend.at[target], mrecv.at[me], msend_sem, mrecv_sem),
            (vsend.at[cap_rows(target)], vrecv.at[cap_rows(me)], vsend_sem, vrecv_sem),
        ):
            copy = pltpu.make_async_remote_copy(
                src_ref=src,
                dst_ref=dst,
                send_sem=ssem.at[off],
                recv_sem=rsem.at[off],
                device_id=dev_id(target),
                device_id_type=MESH,
            )
            copy.start()
            vcopies.append(copy)
    mrecv[pl.ds(me, 1)] = msend[pl.ds(me, 1)]
    vrecv[cap_rows(me), :] = vsend[cap_rows(me), :]

    ring_step(1)
    for k in range(2, far - 1):
        ring_step(k)

    for copy in vcopies:
        copy.wait_recv()
    added = jnp.zeros((tok, half), F32)
    for g in range(n * cap // LANES):
        slot_row = sum([mrecv[s, 0:1, :] for s in range(g * per, (g + 1) * per)])
        hit = lax.broadcasted_iota(jnp.int32, (tok, LANES), 0) + 1 == slot_row
        added += jnp.dot(
            jnp.where(hit, 1.0, 0.0).astype(BF16),
            vrecv[pl.ds(g * LANES, LANES), :],
            preferred_element_type=F32,
        )
    emb[pl.ds(pair, 1)] = (text_ref[...].astype(F32) + added).astype(BF16)[None]
    pair_copy = pltpu.make_async_remote_copy(
        src_ref=emb.at[pair],
        dst_ref=emb.at[pair],
        send_sem=psend_sem,
        recv_sem=precv_sem,
        device_id=other_pair,
        device_id_type=MESH,
    )
    pair_copy.start()

    for s in range(n):
        mask[:, s * tok : (s + 1) * tok] = jnp.where(
            mrecv[s, 1:2, :] <= pos_col, 0.0, -1e30
        )

    ring_step(far - 1)

    pair_copy.wait_recv()
    squares = jnp.zeros((tok, 1), F32)
    for d in range(n):
        floats = emb[d // (n // 2), :, pl.ds(d % (n // 2) * shard, shard)].astype(F32)
        squares += jnp.sum(floats * floats, axis=1, keepdims=True)
    scale = lax.rsqrt(squares / (2 * half) + 1e-6)
    for d in range(n):
        floats = emb[d // (n // 2), :, pl.ds(d % (n // 2) * shard, shard)].astype(F32)
        gain = gain_ref[:, pl.ds(d * shard, shard)].astype(F32)
        nbuf[d] = (floats * scale * gain).astype(BF16)

    local.wait()
    acc = jnp.dot(nbuf[me], wbuf[me], preferred_element_type=F32)

    def projected(total, steps):
        for step in steps:
            for part in range(2):
                ycopies[part, step].wait_recv()
            d = ring_device(lax.rem(where - step + n, n), n)
            total += jnp.dot(nbuf[d], wbuf[d], preferred_element_type=F32)
        return total

    near = [k for step in range(1, far - 1) for k in (step, n - step)]
    acc = projected(acc, near)
    ring_step(far)
    acc = projected(acc, (far - 1, far + 1, far))
    kv = (acc + bias_ref[...].astype(F32)).astype(BF16)
    kvbuf[pl.ds(me, 1)] = kv[None]

    first, second = pl.ds(0, tok // 2), pl.ds(tok // 2, tok // 2)
    kstreams = (
        (first, 1, n // 2),
        (first, -1, n // 2 - 1),
        (second, 1, n // 2 - 1),
        (second, -1, n // 2),
    )
    khops = [
        [
            hop(kvbuf, None, rows, way, k, ksend_sem.at[i, k], krecv_sem.at[i, k])
            for k in range(hops)
        ]
        for i, (rows, way, hops) in enumerate(kstreams)
    ]
    for k in range(n // 2 + 1):
        for i, (rows, way, hops) in enumerate(kstreams):
            if k > hops:
                continue
            if k:
                khops[i][k - 1].wait_recv()
            if k < hops:
                khops[i][k].start()
        if k == 0:
            line = lax.broadcasted_iota(jnp.int32, (tok, tok), 1)
            pick = page_col == line
            cache_ref[...] = jnp.dot(
                jnp.where(pick, 1.0, 0.0).astype(BF16), kv, preferred_element_type=F32
            ).astype(BF16)

    heads = kv.shape[1] // (2 * HD)
    group = query_ref.shape[1] // (HD * heads)
    for head in range(heads):
        keys = kvbuf[:, :, head * 2 * HD : head * 2 * HD + HD].reshape(n * tok, HD)
        values = kvbuf[:, :, head * 2 * HD + HD : (head + 1) * 2 * HD].reshape(n * tok, HD)

        def one(j, carry, head=head, keys=keys, values=values):
            span = pl.ds(pl.multiple_of((head * group + j) * HD, HD), HD)
            scores = lax.dot_general(
                query_ref[:, span], keys, (((1,), (1,)), ((), ())), preferred_element_type=F32
            )
            scores = scores * HD ** (-0.5) + mask[...]
            peak = jnp.max(scores, axis=1, keepdims=True)
            weights = jnp.exp(scores - peak)
            total = jnp.sum(weights, axis=1, keepdims=True)
            mixed = jnp.dot(weights.astype(BF16), values, preferred_element_type=F32)
            out_ref[:, span] = (mixed / total).astype(BF16)
            return carry

        lax.fori_loop(0, group, one, 0, unroll=8 if n <= 8 else 1)

    for hops in whops + khops:
        for copy in hops:
            copy.wait_send()
    for copy in list(ycopies.values()) + vcopies + [pair_copy]:
        copy.wait_send()


def local(
    text_rows,
    vision_rows,
    vision_device,
    vision_slot,
    positions,
    norm_gain,
    kv_weight,
    kv_bias,
    queries,
    page_table,
):
    n = lax.axis_size("dev")
    tok, half = text_rows.shape
    nvis = vision_rows.shape[0]
    shard, columns = kv_weight.shape
    cap = max(16, 2 * nvis // n)
    pages = page_table.shape[1]
    dma = pltpu.SemaphoreType.DMA
    attended, cache = pl.pallas_call(
        functools.partial(kernel, n, cap),
        out_shape=(
            jax.ShapeDtypeStruct(queries.shape, BF16),
            jax.ShapeDtypeStruct((tok, columns), BF16),
        ),
        in_specs=[pl.BlockSpec(memory_space=pltpu.VMEM)] * 10,
        out_specs=(pl.BlockSpec(memory_space=pltpu.VMEM),) * 2,
        scratch_shapes=[
            pltpu.VMEM((n, shard, columns), BF16),
            pltpu.VMEM((n * cap, half), BF16),
            pltpu.VMEM((n * cap, half), BF16),
            pltpu.VMEM((n, 8, LANES), jnp.int32),
            pltpu.VMEM((n, 8, LANES), jnp.int32),
            pltpu.VMEM((2, tok, half), BF16),
            pltpu.VMEM((n, tok, shard), BF16),
            pltpu.VMEM((n, tok, columns), BF16),
            pltpu.VMEM((tok, n * tok), F32),
            dma,
            dma((8, n)),
            dma((8, n)),
            dma((2, n)),
            dma((2, n)),
            dma((n,)),
            dma((n,)),
            dma((n,)),
            dma((n,)),
            dma,
            dma,
            dma((4, n)),
            dma((4, n)),
        ],
        compiler_params=pltpu.CompilerParams(
            collective_id=0, has_side_effects=True, vmem_limit_bytes=60 * 1024 * 1024
        ),
    )(
        text_rows,
        vision_rows,
        vision_device.reshape(1, nvis),
        vision_slot.reshape(1, nvis),
        positions.reshape(1, tok),
        page_table,
        norm_gain.reshape(1, -1),
        kv_bias.reshape(1, -1),
        kv_weight,
        queries,
    )
    return (attended, cache.reshape(pages, PAGE, columns))


def solution(mesh):
    placed = (
        P(("replica", "dev"), "pair"),
        P(("replica", "dev"), "pair"),
        P(("replica", "dev"), None),
        P(("replica", "dev")),
        P(("replica", "dev")),
        P(),
        P("dev", "pair"),
        P("pair"),
        P(("replica", "dev"), "pair"),
        P(("replica", "dev"), None),
    )
    return jax.shard_map(
        local,
        mesh=mesh,
        in_specs=placed,
        out_specs=(P(("replica", "dev"), "pair"), P(("replica", "dev"), None, "pair")),
        check_vma=False,
    )
```
